32 devices in a mesh: region: 2 (over y), mod: 4 (over z), obs: 4 (over x, core).
Axes of the slice: x: 2, y: 2, z: 4, core: 2. Of those that a mesh axis runs over, the one named last changes fastest.
Arguments:
- model_days: float32 [16384, 128], P(('region', 'mod')), parts along dimension 0, may hold values from -48 to 48
- obs_days: float32 [16384, 128], P(('region', 'obs', 'mod')), parts along dimension 0, may hold values from -48 to 48
Outputs:
- mapped: float32 [16384, 128], P(('region', 'mod', 'obs')), parts along dimension 0
- row_potential: float32 [16384], P(('region', 'mod')), parts along dimension 0
- col_potential: float32 [16384], P(('region', 'obs')), parts along dimension 0
The draws below stay inside these ranges and needn't reach their ends.
There are 2 independent parts, one for each index of `region`. The reference program is written for one: setup_inputs(seed, part) draws one part's arguments, and reference() takes and returns one part's arrays. A program takes and returns all parts, laid end to end along the dimension named above; each array names one. Nothing has to cross between parts.
All inputs are finite; a program needn't handle non-finite values.
Results may differ from the reference program's by a relative error of at most 0.0003.
Values sent between devices are 32-bit elements; how exact they have to be, the bound alone decides.
A program may use at most 64 MiB of HBM per device.

```python
import math
import jax
import jax.numpy as jnp
from jax import lax

FEAT = 128
ROWS_DEV = 2048
ITERS = 2
MODEL_DAYS = 8192
OBS_DAYS = 8192
N_MOD = 4


def draw_model_days(key, part):
    base = jax.random.normal(jax.random.fold_in(key, 11), (MODEL_DAYS, FEAT), jnp.float32)
    return base


def draw_obs_days(key, part):
    base = jax.random.normal(jax.random.fold_in(key, 21), (OBS_DAYS, FEAT), jnp.float32)
    return 1.2 * base + 0.3


def setup_inputs(seed: int = 0, part: int = 0) -> dict:
    streams_of = jax.random.split(jax.random.key(seed), 3)
    own_keys = jax.random.split(jax.random.fold_in(streams_of[2], part), 3)
    model_days = draw_model_days(jax.random.fold_in(jax.random.fold_in(streams_of[2], part), 71), part)
    obs_days = draw_obs_days(jax.random.fold_in(jax.random.fold_in(streams_of[2], part), 71), part)
    return dict(model_days=model_days, obs_days=obs_days)


entropy_scale = 0.02


def pair_cost(block_rows, block_square, columns, column_square):
    cross = lax.dot_general(block_rows, columns, (((1,), (1,)), ((), ())), precision=lax.Precision.HIGHEST, preferred_element_type=jnp.float32)
    return (block_square[:, None] + column_square[None, :] - 2.0 * cross) / block_rows.shape[1]


def reference(model_days, obs_days):
    blocks = model_days.reshape(N_MOD, ROWS_DEV, FEAT)
    column_square = jnp.sum(obs_days * obs_days, axis=1)

    def scores_for(block_rows, col_potential):
        block_cost = pair_cost(block_rows, jnp.sum(block_rows * block_rows, axis=1), obs_days, column_square)
        return (col_potential[None, :] - block_cost) / entropy_scale

    def row_lse(col_potential):
        def single(block_rows):
            scores = scores_for(block_rows, col_potential)
            peaks = jnp.max(scores, axis=1)
            return peaks + jnp.log(jnp.sum(jnp.exp(scores - peaks[:, None]), axis=1))
        return lax.map(single, blocks).reshape(-1)

    def col_lse(row_potential):
        potential_blocks = row_potential.reshape(N_MOD, ROWS_DEV)

        def advance(running, inputs):
            block_rows, block_potential = inputs
            block_cost = pair_cost(block_rows, jnp.sum(block_rows * block_rows, axis=1), obs_days, column_square)
            scores = (block_potential[:, None] - block_cost) / entropy_scale
            peaks, totals = running
            new_peaks = jnp.maximum(peaks, jnp.max(scores, axis=0))
            totals = totals * jnp.exp(peaks - new_peaks) + jnp.sum(jnp.exp(scores - new_peaks[None, :]), axis=0)
            return (new_peaks, totals), None

        start = (jnp.full((OBS_DAYS,), -jnp.inf, jnp.float32), jnp.zeros((OBS_DAYS,), jnp.float32))
        (peaks, totals), _ = lax.scan(advance, start, (blocks, potential_blocks))
        return peaks + jnp.log(totals)

    col_potential = jnp.zeros((OBS_DAYS,), jnp.float32)
    for iteration in range(ITERS):
        row_potential = -entropy_scale * (row_lse(col_potential) - math.log(OBS_DAYS))
        col_potential = -entropy_scale * (col_lse(row_potential) - math.log(MODEL_DAYS))
    final_lse = row_lse(col_potential)
    row_potential = -entropy_scale * (final_lse - math.log(OBS_DAYS))

    def project(inputs):
        block_rows, block_lse = inputs
        weights = jnp.exp(scores_for(block_rows, col_potential) - block_lse[:, None])
        return jnp.dot(weights, obs_days, precision=lax.Precision.HIGHEST, preferred_element_type=jnp.float32)

    mapped = lax.map(project, (blocks, final_lse.reshape(N_MOD, ROWS_DEV))).reshape(MODEL_DAYS, FEAT)
    return (mapped, row_potential, col_potential)
```

```python
import functools
import math

import jax
import jax.numpy as jnp
from jax import lax
from jax.experimental import pallas as pl
from jax.experimental.pallas import tpu as pltpu
from jax.sharding import PartitionSpec as P

ITERS = 2
EPS = 0.02
LOG2E = math.log2(math.e)
LN2 = math.log(2.0)
LANE = 128
F32 = jnp.float32
BF16 = jnp.bfloat16


def split3(x):
    a = x.astype(BF16)
    r = x - a.astype(F32)
    b = r.astype(BF16)
    c = (r - b.astype(F32)).astype(BF16)
    return a, b, c


def log2(x):
    return jnp.log(x) * LOG2E


def to_col(row):
    return jnp.broadcast_to(row, (LANE, LANE)).T


def kernel(n_mod, n_obs, model_ref, obs_ref, map_ref, rowp_ref, colp_ref,
           gath, a_ref, b_ref, c_ref, s_ref, q0_ref, q1_ref, w_ref, peak_col,
           tot_col, l_col, rsq, l1_ref, m_ref, v_ref, xrow, xcol, part, mapx,
           g_send, g_recv, r_send, r_recv, c_send, c_recv, p_send, p_recv):
    rows, feat = model_ref.shape
    depth = obs_ref.shape[0]
    cols = depth * n_mod
    nrb, nct, dt = rows // LANE, cols // LANE, depth // LANE
    scale = LOG2E / EPS
    log_obs = math.log2(cols * n_obs)
    log_mod = math.log2(rows * n_mod)
    me_m, me_o = lax.axis_index("mod"), lax.axis_index("obs")
    mod_peer = lambda k: {"mod": lax.rem(me_m + k, n_mod)}
    obs_peer = lambda k: {"obs": lax.rem(me_o + k, n_obs)}

    barrier = pltpu.get_barrier_semaphore()
    for k in range(1, n_mod):
        pl.semaphore_signal(barrier, inc=1, device_id=mod_peer(k), device_id_type=pl.DeviceIdType.MESH)
    for k in range(1, n_obs):
        pl.semaphore_signal(barrier, inc=1, device_id=obs_peer(k), device_id_type=pl.DeviceIdType.MESH)
    pl.semaphore_wait(barrier, n_mod + n_obs - 2)

    def remote(src, dst, send, recv, peer):
        return pltpu.make_async_remote_copy(
            src_ref=src, dst_ref=dst, send_sem=send, recv_sem=recv,
            device_id=peer, device_id_type=pl.DeviceIdType.MESH)

    near = [k // 2 + 1 if k % 2 == 0 else n_mod - (k + 1) // 2 for k in range(n_mod - 1)]
    gathers = {}
    for k in near:
        gathers[k] = remote(obs_ref, gath.at[me_m], g_send.at[k], g_recv.at[k], mod_peer(k))
        gathers[k].start()

    @pl.loop(0, nrb)
    def _(b):
        blk = model_ref[pl.ds(pl.multiple_of(b * LANE, LANE), LANE), :]
        sq = blk * blk
        rsq[pl.ds(b, 1), :] = jnp.sum(sq.T, axis=0, keepdims=True) * (scale / feat)
        p0, p1, p2 = split3(blk * (2.0 * scale / feat))
        at = pl.ds(pl.multiple_of(b * LANE, LANE), LANE)
        for t, piece in enumerate((p0, p0, p1, p1, p0, p2)):
            a_ref[at, t * feat:(t + 1) * feat] = piece

    gath[me_m] = obs_ref[...]

    mrows = math.gcd(rows, 512)
    for step, k in enumerate([0] + near):
        if k:
            gathers[k].wait_recv()
        owner = lax.rem(me_m + n_mod - k, n_mod)
        for t in range(dt):
            bt = gath[owner, t * LANE:(t + 1) * LANE, :].T
            lanes = slice(t * LANE, (t + 1) * LANE)
            c_ref[:, lanes] = jnp.sum(bt * bt, axis=0, keepdims=True) * (scale / feat)
            p0, p1, p2 = split3(bt)
            for u, piece in enumerate((p0, p1, p0, p1, p2, p0)):
                b_ref[u * feat:(u + 1) * feat, lanes] = piece

        @pl.loop(0, rows // mrows)
        def _(b, owner=owner, step=step):
            at = pl.ds(pl.multiple_of(b * mrows, mrows), mrows)
            x = jnp.dot(a_ref[at, :], b_ref[...], preferred_element_type=F32) - c_ref[...]
            for t in range(dt):
                s_ref[owner * dt + t, at, :] = x[:, t * LANE:(t + 1) * LANE]

        chunk = 64

        @pl.loop(0, rows // chunk)
        def _(b, owner=owner, step=step):
            at = pl.ds(pl.multiple_of(b * chunk, chunk), chunk)
            tiles = [s_ref[owner * dt + t, at, :] for t in range(dt)]
            top = functools.reduce(jnp.maximum, tiles)
            top = jnp.broadcast_to(jnp.max(top, axis=1, keepdims=True), (chunk, LANE))
            if step:
                old = peak_col[at, :]
                top = jnp.maximum(top, old)
            total = functools.reduce(jnp.add, [jnp.exp2(t - top) for t in tiles])
            if step:
                total = total + tot_col[at, :] * jnp.exp2(old - top)
            peak_col[at, :] = top
            tot_col[at, :] = total

    def start_rows(e):
        copies = []
        for k in range(1, n_obs):
            copies.append(remote(xrow.at[e, me_o], xrow.at[e, me_o], r_send.at[e, k], r_recv.at[e, k], obs_peer(k)))
            copies[-1].start()
        return copies

    def start_cols(e):
        copies = []
        for k in range(1, n_mod):
            copies.append(remote(xcol.at[e, me_m], xcol.at[e, me_m], c_send.at[e, k], c_recv.at[e, k], mod_peer(k)))
            copies[-1].start()
        return copies

    def finish(copies):
        for copy in copies:
            copy.wait_recv()
        for copy in copies:
            copy.wait_send()

    def lse_over(buf, e, n):
        values = [buf[e, d] for d in range(n)]
        top = functools.reduce(jnp.maximum, values)
        return top + log2(functools.reduce(jnp.add, [jnp.exp2(v - top) for v in values]))

    def sum_over(buf, e, n):
        return functools.reduce(jnp.add, [buf[e, d] for d in range(n)])

    def spread(value_ref):
        @pl.loop(0, nrb)
        def _(b):
            l_col[pl.ds(pl.multiple_of(b * LANE, LANE), LANE), :] = to_col(value_ref[pl.ds(b, 1), :])

    @pl.loop(0, nrb)
    def _(b):
        at = pl.ds(pl.multiple_of(b * LANE, LANE), LANE)
        total = jnp.sum(tot_col[at, :].T, axis=0, keepdims=True)
        xrow[0, me_o, pl.ds(b, 1), :] = peak_col[at, :].T[0:1, :] + log2(total)

    finish(start_rows(0))
    l1_ref[...] = lse_over(xrow, 0, n_obs)
    spread(l1_ref)

    group = 4
    chunk = 64

    def fold(x, op):
        return op(x.reshape(chunk // 8, 8, LANE), axis=0)

    @pl.loop(0, nct // group)
    def _(g):
        def peaks(b, acc):
            at = pl.ds(pl.multiple_of(b * chunk, chunk), chunk)
            l = l_col[at, :]
            return tuple(jnp.maximum(acc[t], fold(s_ref[g * group + t, at, :] - l, jnp.max)) for t in range(group))

        acc = lax.fori_loop(0, rows // chunk, peaks, (jnp.full((8, LANE), -jnp.inf, F32),) * group)
        top = [jnp.max(a, axis=0, keepdims=True) for a in acc]

        def sums(b, acc):
            at = pl.ds(pl.multiple_of(b * chunk, chunk), chunk)
            l = l_col[at, :]
            out = []
            for t in range(group):
                q = jnp.exp2(s_ref[g * group + t, at, :] - l - top[t])
                s_ref[g * group + t, at, :] = q
                out.append(acc[t] + fold(q, jnp.sum))
            return tuple(out)

        acc = lax.fori_loop(0, rows // chunk, sums, (jnp.zeros((8, LANE), F32),) * group)
        for t in range(group):
            m_ref[pl.ds(g * group + t, 1), :] = top[t]
            total = jnp.sum(acc[t], axis=0, keepdims=True)
            xcol[0, me_m, pl.ds(g * group + t, 1), :] = top[t] + log2(total)

    finish(start_cols(0))
    g_all = lse_over(xcol, 0, n_mod)
    v_ref[...] = jnp.exp2(m_ref[...] - g_all)

    def row_totals(e):
        @pl.loop(0, nrb)
        def _(b):
            at = pl.ds(pl.multiple_of(b * LANE, LANE), LANE)
            acc = s_ref[0, at, :] * v_ref[0:1, :]
            for t in range(1, nct):
                acc = acc + s_ref[t, at, :] * v_ref[t:t + 1, :]
            xrow[e, me_o, pl.ds(b, 1), :] = jnp.sum(acc.T, axis=0, keepdims=True)

    for it in range(1, ITERS):
        row_totals(it)
        copies = start_rows(it)
        if it == 1:
            @pl.loop(0, rows // chunk)
            def _(b):
                at = pl.ds(pl.multiple_of(b * chunk, chunk), chunk)
                for t in range(nct):
                    q = s_ref[t, at, :]
                    hi = q.astype(BF16)
                    q0_ref[at, t * LANE:(t + 1) * LANE] = hi
                    q1_ref[at, t * LANE:(t + 1) * LANE] = (q - hi.astype(F32)).astype(BF16)
        finish(copies)
        rsum = sum_over(xrow, it, n_obs)
        xrow[it, me_o] = 1.0 / rsum

        @pl.loop(0, nrb)
        def _(b, it=it):
            l_col[pl.ds(pl.multiple_of(b * LANE, LANE), LANE), :] = to_col(xrow[it, me_o, pl.ds(b, 1), :])

        @pl.loop(0, nct // group)
        def _(g, it=it):
            def sums(b, acc):
                at = pl.ds(pl.multiple_of(b * chunk, chunk), chunk)
                u = l_col[at, :]
                return tuple(acc[t] + fold(s_ref[g * group + t, at, :] * u, jnp.sum) for t in range(group))

            acc = lax.fori_loop(0, rows // chunk, sums, (jnp.zeros((8, LANE), F32),) * group)
            for t in range(group):
                ct = pl.ds(g * group + t, 1)
                xcol[it, me_m, ct, :] = jnp.sum(acc[t], axis=0, keepdims=True) * v_ref[ct, :]

        finish(start_cols(it))
        csum = sum_over(xcol, it, n_mod)
        v_ref[...] = v_ref[...] / csum
        g_all = g_all + log2(csum)

    colp_ref[...] = (ITERS * (log_mod - log_obs) - g_all) * (EPS * LN2)
    row_totals(ITERS)
    last = start_rows(ITERS)

    @pl.loop(0, nct)
    def _(t):
        at = pl.ds(pl.multiple_of(t * LANE, LANE), LANE)
        o = gath[t // dt, pl.ds(pl.multiple_of(lax.rem(t, dt) * LANE, LANE), LANE), :]
        w = o * to_col(v_ref[pl.ds(t, 1), :])
        hi = w.astype(BF16)
        w_ref[at, 0:feat] = hi
        w_ref[at, feat:2 * feat] = (w - hi.astype(F32)).astype(BF16)

    share = rows // n_obs

    def project(owner):
        at = pl.ds(pl.multiple_of(owner * share, share), share)
        y = jnp.dot(q0_ref[at, :], w_ref[...], preferred_element_type=F32)
        y = y + jnp.dot(q1_ref[at, :], w_ref[...], preferred_element_type=F32)
        return y[:, :feat] + y[:, feat:]

    sends = []
    for k in range(1, n_obs):
        part[k - 1] = project(lax.rem(me_o + k, n_obs))
        sends.append(remote(part.at[k - 1], mapx.at[k - 1], p_send.at[k], p_recv.at[k], obs_peer(k)))
        sends[-1].start()
    map_ref[...] = project(me_o)

    finish(last)
    rsum = sum_over(xrow, ITERS, n_obs)
    rowp_ref[...] = (log_obs - ITERS * (log_mod - log_obs) - l1_ref[...] - log2(rsum) + rsq[...]) * (EPS * LN2)
    l1_ref[...] = 1.0 / rsum
    for k in range(1, n_obs):
        sends[k - 1].wait_recv()
    for b in range(share // LANE):
        at = slice(b * LANE, (b + 1) * LANE)
        y = map_ref[at, :]
        for k in range(1, n_obs):
            y = y + mapx[k - 1, at, :]
        map_ref[at, :] = y * to_col(l1_ref[pl.ds(me_o * (share // LANE) + b, 1), :])
    for k in range(1, n_obs):
        sends[k - 1].wait_send()
    for k in near:
        gathers[k].wait_send()


def on_device(n_mod, n_obs, model_days, obs_days):
    rows, feat = model_days.shape
    depth = obs_days.shape[0]
    cols = depth * n_mod
    share = rows // n_obs
    nrb, nct = rows // LANE, cols // LANE
    vmem = pl.BlockSpec(memory_space=pltpu.VMEM)
    dma = pltpu.SemaphoreType.DMA
    mapped, rowp, colp = pl.pallas_call(
        functools.partial(kernel, n_mod, n_obs),
        out_shape=(
            jax.ShapeDtypeStruct((share, feat), F32),
            jax.ShapeDtypeStruct((nrb, LANE), F32),
            jax.ShapeDtypeStruct((nct, LANE), F32),
        ),
        in_specs=[vmem, vmem],
        out_specs=(vmem, vmem, vmem),
        scratch_shapes=[
            pltpu.VMEM((n_mod, depth, feat), F32),
            pltpu.VMEM((rows, 6 * feat), BF16),
            pltpu.VMEM((6 * feat, depth), BF16),
            pltpu.VMEM((1, depth), F32),
            pltpu.VMEM((nct, rows, LANE), F32),
            pltpu.VMEM((rows, cols), BF16),
            pltpu.VMEM((rows, cols), BF16),
            pltpu.VMEM((cols, 2 * feat), BF16),
            pltpu.VMEM((rows, LANE), F32),
            pltpu.VMEM((rows, LANE), F32),
            pltpu.VMEM((rows, LANE), F32),
            pltpu.VMEM((nrb, LANE), F32),
            pltpu.VMEM((nrb, LANE), F32),
            pltpu.VMEM((nct, LANE), F32),
            pltpu.VMEM((nct, LANE), F32),
            pltpu.VMEM((ITERS + 1, n_obs, nrb, LANE), F32),
            pltpu.VMEM((ITERS, n_mod, nct, LANE), F32),
            pltpu.VMEM((n_obs - 1, share, feat), F32),
            pltpu.VMEM((n_obs - 1, share, feat), F32),
            dma((n_mod,)), dma((n_mod,)),
            dma((ITERS + 1, n_obs)), dma((ITERS + 1, n_obs)),
            dma((ITERS, n_mod)), dma((ITERS, n_mod)),
            dma((n_obs,)), dma((n_obs,)),
        ],
        compiler_params=pltpu.CompilerParams(
            collective_id=0, has_side_effects=True, vmem_limit_bytes=56 * 1024 * 1024),
        cost_estimate=pl.CostEstimate(
            flops=20 * rows * cols * feat, bytes_accessed=8 * rows * feat, transcendentals=3 * rows * cols),
    )(model_days, obs_days)
    return mapped, rowp.reshape(rows), colp.reshape(cols)


def solution(mesh):
    n_mod, n_obs = mesh.shape["mod"], mesh.shape["obs"]
    in_specs = (P(("region", "mod"), None), P(("region", "obs", "mod"), None))
    out_specs = (P(("region", "mod", "obs"), None), P(("region", "mod")), P(("region", "obs")))
    return jax.shard_map(
        functools.partial(on_device, n_mod, n_obs), mesh=mesh,
        in_specs=in_specs, out_specs=out_specs, check_vma=False,
    )
```

```python
import functools
import math

import jax
import jax.numpy as jnp
from jax import lax
from jax.experimental import pallas as pl
from jax.experimental.pallas import tpu as pltpu
from jax.sharding import PartitionSpec as P

ITERS = 2
EPS = 0.02
LOG2E = math.log2(math.e)
LN2 = math.log(2.0)
LANE = 128
F32 = jnp.float32
BF16 = jnp.bfloat16


def split3(x):
    a = x.astype(BF16)
    r = x - a.astype(F32)
    b = r.astype(BF16)
    c = (r - b.astype(F32)).astype(BF16)
    return a, b, c


def log2(x):
    return jnp.log(x) * LOG2E


def to_col(row):
    return jnp.broadcast_to(row, (LANE, LANE)).T


def kernel(n_mod, n_obs, model_ref, obs_ref, map_ref, rowp_ref, colp_ref,
           gath, a_ref, b_ref, c_ref, s_ref, q0_ref, q1_ref, w_ref, peak_col,
           tot_col, l_col, rsq, l1_ref, m_ref, v_ref, xrow, xcol, part, half, keep, mapx,
           g_send, g_recv, r_send, r_recv, c_send, c_recv, p_send, p_recv):
    rows, feat = model_ref.shape
    depth = obs_ref.shape[0]
    cols = depth * n_mod
    nrb, nct, dt = rows // LANE, cols // LANE, depth // LANE
    scale = LOG2E / EPS
    log_obs = math.log2(cols * n_obs)
    log_mod = math.log2(rows * n_mod)
    me_m, me_o = lax.axis_index("mod"), lax.axis_index("obs")
    mod_peer = lambda k: {"mod": lax.rem(me_m + k, n_mod)}
    obs_peer = lambda k: {"obs": lax.rem(me_o + k, n_obs)}

    barrier = pltpu.get_barrier_semaphore()
    for k in range(1, n_mod):
        pl.semaphore_signal(barrier, inc=1, device_id=mod_peer(k), device_id_type=pl.DeviceIdType.MESH)
    for k in range(1, n_obs):
        pl.semaphore_signal(barrier, inc=1, device_id=obs_peer(k), device_id_type=pl.DeviceIdType.MESH)
    def remote(src, dst, send, recv, peer):
        return pltpu.make_async_remote_copy(
            src_ref=src, dst_ref=dst, send_sem=send, recv_sem=recv,
            device_id=peer, device_id_type=pl.DeviceIdType.MESH)

    @pl.loop(0, nrb)
    def _(b):
        blk = model_ref[pl.ds(pl.multiple_of(b * LANE, LANE), LANE), :]
        sq = blk * blk
        rsq[pl.ds(b, 1), :] = jnp.sum(sq.T, axis=0, keepdims=True) * (scale / feat)
        p0, p1, p2 = split3(blk * (2.0 * scale / feat))
        at = pl.ds(pl.multiple_of(b * LANE, LANE), LANE)
        for t, piece in enumerate((p0, p0, p1, p1, p0, p2)):
            a_ref[at, t * feat:(t + 1) * feat] = piece

    pl.semaphore_wait(barrier, n_mod + n_obs - 2)

    right, left = {"mod": lax.rem(me_m + 1, n_mod)}, {"mod": lax.rem(me_m + n_mod - 1, n_mod)}
    has_right, has_left = me_m < n_mod - 1, me_m > 0
    inside = jnp.logical_and(has_right, has_left)
    n_left, n_right = me_m, n_mod - 1 - me_m
    both = jnp.minimum(n_left, n_right)

    def block_at(j):
        paired = (j - 1) < 2 * both
        far = jnp.where(paired, (j - 1) // 2 + 1, j - both)
        to_left = jnp.where(paired, (j - 1) % 2 == 0, n_left > n_right)
        return jnp.where(to_left, me_m - far, me_m + far)

    def own_to(peer, sem):
        return remote(obs_ref, gath.at[me_m], g_send.at[sem], g_recv.at[me_m], peer)

    def pass_on(block, peer):
        return remote(gath.at[block], gath.at[block], g_send.at[block], g_recv.at[block], peer)

    def each_send(block, act):
        @pl.when(jnp.logical_and(block < me_m, has_right))
        def _():
            act(pass_on(block, right))

        @pl.when(jnp.logical_and(block > me_m, has_left))
        def _():
            act(pass_on(block, left))

    def own_sends(act):
        @pl.when(has_right)
        def _():
            act(own_to(right, me_m))

        @pl.when(has_left)
        def _():
            act(own_to(left, n_mod))

    def arrive(j):
        block = block_at(j)
        pass_on(block, right).wait_recv()
        each_send(block, lambda copy: copy.start())

    own_sends(lambda copy: copy.start())
    gath[me_m] = obs_ref[...]

    mrows = math.gcd(rows, 512)
    for step in range(n_mod):
        if step == 1:
            arrive(1)
        if step and step + 1 < n_mod:
            pl.when(inside)(functools.partial(arrive, step + 1))
        owner = block_at(step) if step else me_m
        for t in range(dt):
            bt = gath[owner, t * LANE:(t + 1) * LANE, :].T
            lanes = slice(t * LANE, (t + 1) * LANE)
            c_ref[:, lanes] = jnp.sum(bt * bt, axis=0, keepdims=True) * (scale / feat)
            p0, p1, p2 = split3(bt)
            for u, piece in enumerate((p0, p1, p0, p1, p2, p0)):
                b_ref[u * feat:(u + 1) * feat, lanes] = piece

        @pl.loop(0, rows // mrows)
        def _(b, owner=owner, step=step):
            at = pl.ds(pl.multiple_of(b * mrows, mrows), mrows)
            x = jnp.dot(a_ref[at, :], b_ref[...], preferred_element_type=F32) - c_ref[...]
            for t in range(dt):
                s_ref[owner * dt + t, at, :] = x[:, t * LANE:(t + 1) * LANE]

        chunk = 64

        @pl.loop(0, rows // chunk, unroll=2)
        def _(b, owner=owner, step=step):
            at = pl.ds(pl.multiple_of(b * chunk, chunk), chunk)
            tiles = [s_ref[owner * dt + t, at, :] for t in range(dt)]
            top = functools.reduce(jnp.maximum, tiles)
            if step:
                old = peak_col[at, :]
                top = jnp.maximum(top, old)
            total = functools.reduce(jnp.add, [jnp.exp2(t - top) for t in tiles])
            if step:
                total = total + tot_col[at, :] * jnp.exp2(old - top)
            peak_col[at, :] = top
            tot_col[at, :] = total

        if step and step + 1 < n_mod:
            pl.when(jnp.logical_not(inside))(functools.partial(arrive, step + 1))

    def start_rows(e):
        copies = []
        for k in range(1, n_obs):
            copies.append(remote(xrow.at[e, me_o], xrow.at[e, me_o], r_send.at[e, k], r_recv.at[e, k], obs_peer(k)))
            copies[-1].start()
        return copies

    def start_cols(e):
        copies = []
        for k in range(1, n_mod):
            copies.append(remote(xcol.at[e, me_m], xcol.at[e, me_m], c_send.at[e, k], c_recv.at[e, k], mod_peer(k)))
            copies[-1].start()
        return copies

    def finish(copies):
        for copy in copies:
            copy.wait_recv()
        for copy in copies:
            copy.wait_send()

    def lse_over(buf, e, n):
        values = [buf[e, d] for d in range(n)]
        top = functools.reduce(jnp.maximum, values)
        return top + log2(functools.reduce(jnp.add, [jnp.exp2(v - top) for v in values]))

    def sum_over(buf, e, n):
        return functools.reduce(jnp.add, [buf[e, d] for d in range(n)])

    def spread(value_ref):
        @pl.loop(0, nrb)
        def _(b):
            l_col[pl.ds(pl.multiple_of(b * LANE, LANE), LANE), :] = to_col(value_ref[pl.ds(b, 1), :])

    @pl.loop(0, nrb)
    def _(b):
        at = pl.ds(pl.multiple_of(b * LANE, LANE), LANE)
        peaks = peak_col[at, :].T
        top = jnp.max(peaks, axis=0, keepdims=True)
        total = jnp.sum(tot_col[at, :].T * jnp.exp2(peaks - top), axis=0, keepdims=True)
        xrow[0, me_o, pl.ds(b, 1), :] = top + log2(total)

    finish(start_rows(0))
    l1_ref[...] = lse_over(xrow, 0, n_obs)
    spread(l1_ref)

    group = 4
    chunk = 128

    def fold(x, op):
        return op(x.reshape(chunk // 8, 8, LANE), axis=0)

    @pl.loop(0, nct // group)
    def _(g):
        def peaks(b, acc):
            at = pl.ds(pl.multiple_of(b * chunk, chunk), chunk)
            l = l_col[at, :]
            return tuple(jnp.maximum(acc[t], fold(s_ref[g * group + t, at, :] - l, jnp.max)) for t in range(group))

        acc = lax.fori_loop(0, rows // chunk, peaks, (jnp.full((8, LANE), -jnp.inf, F32),) * group)
        top = [jnp.max(a, axis=0, keepdims=True) for a in acc]

        def sums(b, acc):
            at = pl.ds(pl.multiple_of(b * chunk, chunk), chunk)
            l = l_col[at, :]
            out = []
            for t in range(group):
                q = jnp.exp2(s_ref[g * group + t, at, :] - l - top[t])
                s_ref[g * group + t, at, :] = q
                out.append(acc[t] + fold(q, jnp.sum))
            return tuple(out)

        acc = lax.fori_loop(0, rows // chunk, sums, (jnp.zeros((8, LANE), F32),) * group)
        for t in range(group):
            m_ref[pl.ds(g * group + t, 1), :] = top[t]
            total = jnp.sum(acc[t], axis=0, keepdims=True)
            xcol[0, me_m, pl.ds(g * group + t, 1), :] = top[t] + log2(total)

    finish(start_cols(0))
    g_all = lse_over(xcol, 0, n_mod)
    v_ref[...] = jnp.exp2(m_ref[...] - g_all)

    def row_totals(e):
        @pl.loop(0, nrb)
        def _(b):
            at = pl.ds(pl.multiple_of(b * LANE, LANE), LANE)
            acc = s_ref[0, at, :] * v_ref[0:1, :]
            for t in range(1, nct):
                acc = acc + s_ref[t, at, :] * v_ref[t:t + 1, :]
            xrow[e, me_o, pl.ds(b, 1), :] = jnp.sum(acc.T, axis=0, keepdims=True)

    for it in range(1, ITERS):
        row_totals(it)
        copies = start_rows(it)
        if it == 1:
            @pl.loop(0, rows // chunk)
            def _(b):
                at = pl.ds(pl.multiple_of(b * chunk, chunk), chunk)
                for t in range(nct):
                    q = s_ref[t, at, :]
                    hi = q.astype(BF16)
                    q0_ref[at, t * LANE:(t + 1) * LANE] = hi
                    q1_ref[at, t * LANE:(t + 1) * LANE] = (q - hi.astype(F32)).astype(BF16)
        finish(copies)
        rsum = sum_over(xrow, it, n_obs)
        xrow[it, me_o] = 1.0 / rsum

        @pl.loop(0, nrb)
        def _(b, it=it):
            l_col[pl.ds(pl.multiple_of(b * LANE, LANE), LANE), :] = to_col(xrow[it, me_o, pl.ds(b, 1), :])

        @pl.loop(0, nct // group)
        def _(g, it=it):
            def sums(b, acc):
                at = pl.ds(pl.multiple_of(b * chunk, chunk), chunk)
                u = l_col[at, :]
                return tuple(acc[t] + fold(s_ref[g * group + t, at, :] * u, jnp.sum) for t in range(group))

            acc = lax.fori_loop(0, rows // chunk, sums, (jnp.zeros((8, LANE), F32),) * group)
            for t in range(group):
                ct = pl.ds(g * group + t, 1)
                xcol[it, me_m, ct, :] = jnp.sum(acc[t], axis=0, keepdims=True) * v_ref[ct, :]

        finish(start_cols(it))
        csum = sum_over(xcol, it, n_mod)
        v_ref[...] = v_ref[...] / csum
        g_all = g_all + log2(csum)

    colp_ref[...] = (ITERS * (log_mod - log_obs) - g_all) * (EPS * LN2)
    row_totals(ITERS)
    last = start_rows(ITERS)

    @pl.loop(0, nct)
    def _(t):
        at = pl.ds(pl.multiple_of(t * LANE, LANE), LANE)
        o = gath[t // dt, pl.ds(pl.multiple_of(lax.rem(t, dt) * LANE, LANE), LANE), :]
        w = o * to_col(v_ref[pl.ds(t, 1), :])
        hi = w.astype(BF16)
        w_ref[at, 0:feat] = hi
        w_ref[at, feat:2 * feat] = (w - hi.astype(F32)).astype(BF16)

    share = rows // n_obs

    def project(owner):
        at = pl.ds(pl.multiple_of(owner * share, share), share)
        y = jnp.dot(q0_ref[at, :], w_ref[...], preferred_element_type=F32)
        y = y + jnp.dot(q1_ref[at, :], w_ref[...], preferred_element_type=F32)
        return y[:, :feat] + y[:, feat:]

    chips = n_obs // 2
    chip, core = me_o // 2, lax.rem(me_o, 2)
    mate = {"obs": chip * 2 + 1 - core}
    halves, sends = [], []
    for d in list(range(1, chips)) + [0]:
        there = lax.rem(chip + d, chips) * 2
        part[d] = project(there + 1 - core)
        halves.append(remote(part.at[d], half.at[d], p_send.at[d], p_recv.at[d], mate))
        halves[-1].start()
        mine = project(there + core)
        if d:
            halves[-1].wait_recv()
            keep[d - 1] = mine + half[d]
            sends.append(remote(keep.at[d - 1], mapx.at[d - 1], p_send.at[chips + d], p_recv.at[chips + d], {"obs": there + core}))
            sends[-1].start()
        else:
            map_ref[...] = mine

    finish(last)
    rsum = sum_over(xrow, ITERS, n_obs)
    rowp_ref[...] = (log_obs - ITERS * (log_mod - log_obs) - l1_ref[...] - log2(rsum) + rsq[...]) * (EPS * LN2)
    l1_ref[...] = 1.0 / rsum
    halves[-1].wait_recv()
    for copy in sends:
        copy.wait_recv()
    for b in range(share // LANE):
        at = slice(b * LANE, (b + 1) * LANE)
        y = map_ref[at, :] + half[0, at, :]
        for d in range(1, chips):
            y = y + mapx[d - 1, at, :]
        map_ref[at, :] = y * to_col(l1_ref[pl.ds(me_o * (share // LANE) + b, 1), :])
    for copy in halves + sends:
        copy.wait_send()
    own_sends(lambda copy: copy.wait_send())
    for step in range(1, n_mod):
        each_send(block_at(step), lambda copy: copy.wait_send())


def on_device(n_mod, n_obs, model_days, obs_days):
    rows, feat = model_days.shape
    depth = obs_days.shape[0]
    cols = depth * n_mod
    share = rows // n_obs
    nrb, nct = rows // LANE, cols // LANE
    vmem = pl.BlockSpec(memory_space=pltpu.VMEM)
    dma = pltpu.SemaphoreType.DMA
    mapped, rowp, colp = pl.pallas_call(
        functools.partial(kernel, n_mod, n_obs),
        out_shape=(
            jax.ShapeDtypeStruct((share, feat), F32),
            jax.ShapeDtypeStruct((nrb, LANE), F32),
            jax.ShapeDtypeStruct((nct, LANE), F32),
        ),
        in_specs=[vmem, vmem],
        out_specs=(vmem, vmem, vmem),
        scratch_shapes=[
            pltpu.VMEM((n_mod, depth, feat), F32),
            pltpu.VMEM((rows, 6 * feat), BF16),
            pltpu.VMEM((6 * feat, depth), BF16),
            pltpu.VMEM((1, depth), F32),
            pltpu.VMEM((nct, rows, LANE), F32),
            pltpu.VMEM((rows, cols), BF16),
            pltpu.VMEM((rows, cols), BF16),
            pltpu.VMEM((cols, 2 * feat), BF16),
            pltpu.VMEM((rows, LANE), F32),
            pltpu.VMEM((rows, LANE), F32),
            pltpu.VMEM((rows, LANE), F32),
            pltpu.VMEM((nrb, LANE), F32),
            pltpu.VMEM((nrb, LANE), F32),
            pltpu.VMEM((nct, LANE), F32),
            pltpu.VMEM((nct, LANE), F32),
            pltpu.VMEM((ITERS + 1, n_obs, nrb, LANE), F32),
            pltpu.VMEM((ITERS, n_mod, nct, LANE), F32),
            pltpu.VMEM((n_obs // 2, share, feat), F32),
            pltpu.VMEM((n_obs // 2, share, feat), F32),
            pltpu.VMEM((n_obs // 2 - 1, share, feat), F32),
            pltpu.VMEM((n_obs // 2 - 1, share, feat), F32),
            dma((n_mod + 1,)), dma((n_mod,)),
            dma((ITERS + 1, n_obs)), dma((ITERS + 1, n_obs)),
            dma((ITERS, n_mod)), dma((ITERS, n_mod)),
            dma((n_obs,)), dma((n_obs,)),
        ],
        compiler_params=pltpu.CompilerParams(
            collective_id=0, has_side_effects=True, vmem_limit_bytes=56 * 1024 * 1024),
        cost_estimate=pl.CostEstimate(
            flops=20 * rows * cols * feat, bytes_accessed=8 * rows * feat, transcendentals=3 * rows * cols),
    )(model_days, obs_days)
    return mapped, rowp.reshape(rows), colp.reshape(cols)


def solution(mesh):
    n_mod, n_obs = mesh.shape["mod"], mesh.shape["obs"]
    in_specs = (P(("region", "mod"), None), P(("region", "obs", "mod"), None))
    out_specs = (P(("region", "mod", "obs"), None), P(("region", "mod")), P(("region", "obs")))
    return jax.shard_map(
        functools.partial(on_device, n_mod, n_obs), mesh=mesh,
        in_specs=in_specs, out_specs=out_specs, check_vma=False,
    )
```

```python
import functools
import math

import jax
import jax.numpy as jnp
from jax import lax
from jax.experimental import pallas as pl
from jax.experimental.pallas import tpu as pltpu
from jax.sharding import PartitionSpec as P

ITERS = 2
EPS = 0.02
LOG2E = math.log2(math.e)
LN2 = math.log(2.0)
LANE = 128
F32 = jnp.float32
BF16 = jnp.bfloat16


def split3(x):
    a = x.astype(BF16)
    r = x - a.astype(F32)
    b = r.astype(BF16)
    c = (r - b.astype(F32)).astype(BF16)
    return a, b, c


def log2(x):
    return jnp.log(x) * LOG2E


def to_col(row):
    return jnp.broadcast_to(row, (LANE, LANE)).T


def kernel(n_mod, n_obs, model_ref, obs_ref, map_ref, rowp_ref, colp_ref,
           gath, a_ref, b_ref, c_ref, s_ref, q0_ref, q1_ref, w_ref, peak_col,
           tot_col, l_col, rsq, l1_ref, m_ref, v_ref, xrow, xcol, part, half, keep, mapx,
           g_send, g_recv, r_send, r_recv, c_send, c_recv, p_send, p_recv):
    rows, feat = model_ref.shape
    depth = obs_ref.shape[0]
    cols = depth * n_mod
    nrb, nct, dt = rows // LANE, cols // LANE, depth // LANE
    scale = LOG2E / EPS
    log_obs = math.log2(cols * n_obs)
    log_mod = math.log2(rows * n_mod)
    me_m, me_o = lax.axis_index("mod"), lax.axis_index("obs")
    mod_peer = lambda k: {"mod": lax.rem(me_m + k, n_mod)}
    obs_peer = lambda k: {"obs": lax.rem(me_o + k, n_obs)}

    barrier = pltpu.get_barrier_semaphore()
    for k in range(1, n_mod):
        pl.semaphore_signal(barrier, inc=1, device_id=mod_peer(k), device_id_type=pl.DeviceIdType.MESH)
    for k in range(1, n_obs):
        pl.semaphore_signal(barrier, inc=1, device_id=obs_peer(k), device_id_type=pl.DeviceIdType.MESH)
    def remote(src, dst, send, recv, peer):
        return pltpu.make_async_remote_copy(
            src_ref=src, dst_ref=dst, send_sem=send, recv_sem=recv,
            device_id=peer, device_id_type=pl.DeviceIdType.MESH)

    @pl.loop(0, nrb)
    def _(b):
        blk = model_ref[pl.ds(pl.multiple_of(b * LANE, LANE), LANE), :]
        sq = blk * blk
        rsq[pl.ds(b, 1), :] = jnp.sum(sq.T, axis=0, keepdims=True) * (scale / feat)
        p0, p1, p2 = split3(blk * (2.0 * scale / feat))
        at = pl.ds(pl.multiple_of(b * LANE, LANE), LANE)
        for t, piece in enumerate((p0, p0, p1, p1, p0, p2)):
            a_ref[at, t * feat:(t + 1) * feat] = piece

    pl.semaphore_wait(barrier, n_mod + n_obs - 2)

    right, left = {"mod": lax.rem(me_m + 1, n_mod)}, {"mod": lax.rem(me_m + n_mod - 1, n_mod)}
    has_right, has_left = me_m < n_mod - 1, me_m > 0
    inside = jnp.logical_and(has_right, has_left)
    n_left, n_right = me_m, n_mod - 1 - me_m
    both = jnp.minimum(n_left, n_right)

    def block_at(j):
        paired = (j - 1) < 2 * both
        far = jnp.where(paired, (j - 1) // 2 + 1, j - both)
        to_left = jnp.where(paired, (j - 1) % 2 == 0, n_left > n_right)
        return jnp.where(to_left, me_m - far, me_m + far)

    def own_to(peer, sem):
        return remote(obs_ref, gath.at[me_m], g_send.at[sem], g_recv.at[me_m], peer)

    def pass_on(block, peer):
        return remote(gath.at[block], gath.at[block], g_send.at[block], g_recv.at[block], peer)

    def each_send(block, act):
        @pl.when(jnp.logical_and(block < me_m, has_right))
        def _():
            act(pass_on(block, right))

        @pl.when(jnp.logical_and(block > me_m, has_left))
        def _():
            act(pass_on(block, left))

    def own_sends(act):
        @pl.when(has_right)
        def _():
            act(own_to(right, me_m))

        @pl.when(has_left)
        def _():
            act(own_to(left, n_mod))

    def arrive(j):
        block = block_at(j)
        pass_on(block, right).wait_recv()
        each_send(block, lambda copy: copy.start())

    own_sends(lambda copy: copy.start())
    gath[me_m] = obs_ref[...]

    mrows = math.gcd(rows, 512)
    for step in range(n_mod):
        if step == 1:
            arrive(1)
        if step and step + 1 < n_mod:
            pl.when(inside)(functools.partial(arrive, step + 1))
        owner = block_at(step) if step else me_m
        for t in range(dt):
            bt = gath[owner, t * LANE:(t + 1) * LANE, :].T
            lanes = slice(t * LANE, (t + 1) * LANE)
            c_ref[:, lanes] = jnp.sum(bt * bt, axis=0, keepdims=True) * (scale / feat)
            p0, p1, p2 = split3(bt)
            for u, piece in enumerate((p0, p1, p0, p1, p2, p0)):
                b_ref[u * feat:(u + 1) * feat, lanes] = piece

        @pl.loop(0, rows // mrows)
        def _(b, owner=owner, step=step):
            at = pl.ds(pl.multiple_of(b * mrows, mrows), mrows)
            x = jnp.dot(a_ref[at, :], b_ref[...], preferred_element_type=F32) - c_ref[...]
            for t in range(dt):
                s_ref[owner * dt + t, at, :] = x[:, t * LANE:(t + 1) * LANE]

        chunk = 64

        @pl.loop(0, rows // chunk, unroll=2)
        def _(b, owner=owner, step=step):
            at = pl.ds(pl.multiple_of(b * chunk, chunk), chunk)
            tiles = [s_ref[owner * dt + t, at, :] for t in range(dt)]
            top = functools.reduce(jnp.maximum, tiles)
            if step:
                old = peak_col[at, :]
                top = jnp.maximum(top, old)
            total = functools.reduce(jnp.add, [jnp.exp2(t - top) for t in tiles])
            if step:
                total = total + tot_col[at, :] * jnp.exp2(old - top)
            peak_col[at, :] = top
            tot_col[at, :] = total

        if step and step + 1 < n_mod:
            pl.when(jnp.logical_not(inside))(functools.partial(arrive, step + 1))

    def start_rows(e):
        copies = []
        for k in range(1, n_obs):
            copies.append(remote(xrow.at[e, me_o], xrow.at[e, me_o], r_send.at[e, k], r_recv.at[e, k], obs_peer(k)))
            copies[-1].start()
        return copies

    def start_cols(e):
        copies = []
        for k in range(1, n_mod):
            copies.append(remote(xcol.at[e, me_m], xcol.at[e, me_m], c_send.at[e, k], c_recv.at[e, k], mod_peer(k)))
            copies[-1].start()
        return copies

    def finish(copies):
        for copy in copies:
            copy.wait_recv()
        for copy in copies:
            copy.wait_send()

    def lse_over(buf, e, n):
        values = [buf[e, d] for d in range(n)]
        top = functools.reduce(jnp.maximum, values)
        return top + log2(functools.reduce(jnp.add, [jnp.exp2(v - top) for v in values]))

    def sum_over(buf, e, n):
        return functools.reduce(jnp.add, [buf[e, d] for d in range(n)])

    def spread(value_ref):
        @pl.loop(0, nrb)
        def _(b):
            l_col[pl.ds(pl.multiple_of(b * LANE, LANE), LANE), :] = to_col(value_ref[pl.ds(b, 1), :])

    @pl.loop(0, nrb)
    def _(b):
        at = pl.ds(pl.multiple_of(b * LANE, LANE), LANE)
        peaks = peak_col[at, :].T
        top = jnp.max(peaks, axis=0, keepdims=True)
        total = jnp.sum(tot_col[at, :].T * jnp.exp2(peaks - top), axis=0, keepdims=True)
        xrow[0, me_o, pl.ds(b, 1), :] = top + log2(total)

    finish(start_rows(0))
    l1_ref[...] = lse_over(xrow, 0, n_obs)
    spread(l1_ref)

    group = 4
    chunk = 128

    def fold(x, op):
        return op(x.reshape(chunk // 8, 8, LANE), axis=0)

    @pl.loop(0, nct // group)
    def _(g):
        def peaks(b, acc):
            at = pl.ds(pl.multiple_of(b * chunk, chunk), chunk)
            l = l_col[at, :]
            return tuple(jnp.maximum(acc[t], fold(s_ref[g * group + t, at, :] - l, jnp.max)) for t in range(group))

        acc = lax.fori_loop(0, rows // chunk, peaks, (jnp.full((8, LANE), -jnp.inf, F32),) * group)
        top = [jnp.max(a, axis=0, keepdims=True) for a in acc]

        def sums(b, acc):
            at = pl.ds(pl.multiple_of(b * chunk, chunk), chunk)
            l = l_col[at, :]
            out = []
            for t in range(group):
                q = jnp.exp2(s_ref[g * group + t, at, :] - l - top[t])
                s_ref[g * group + t, at, :] = q
                out.append(acc[t] + fold(q, jnp.sum))
            return tuple(out)

        acc = lax.fori_loop(0, rows // chunk, sums, (jnp.zeros((8, LANE), F32),) * group)
        for t in range(group):
            m_ref[pl.ds(g * group + t, 1), :] = top[t]
            total = jnp.sum(acc[t], axis=0, keepdims=True)
            xcol[0, me_m, pl.ds(g * group + t, 1), :] = top[t] + log2(total)

    finish(start_cols(0))
    g_all = lse_over(xcol, 0, n_mod)
    v_ref[...] = jnp.exp2(m_ref[...] - g_all)

    def row_totals(e):
        @pl.loop(0, nrb)
        def _(b):
            at = pl.ds(pl.multiple_of(b * LANE, LANE), LANE)
            acc = s_ref[0, at, :] * v_ref[0:1, :]
            for t in range(1, nct):
                acc = acc + s_ref[t, at, :] * v_ref[t:t + 1, :]
            xrow[e, me_o, pl.ds(b, 1), :] = jnp.sum(acc.T, axis=0, keepdims=True)

    for it in range(1, ITERS):
        row_totals(it)
        copies = start_rows(it)
        if it == 1:
            @pl.loop(0, rows // chunk)
            def _(b):
                at = pl.ds(pl.multiple_of(b * chunk, chunk), chunk)
                for t in range(nct):
                    q = s_ref[t, at, :]
                    hi = q.astype(BF16)
                    q0_ref[at, t * LANE:(t + 1) * LANE] = hi
                    q1_ref[at, t * LANE:(t + 1) * LANE] = (q - hi.astype(F32)).astype(BF16)
        finish(copies)
        rsum = sum_over(xrow, it, n_obs)
        xrow[it, me_o] = 1.0 / rsum

        @pl.loop(0, nrb)
        def _(b, it=it):
            l_col[pl.ds(pl.multiple_of(b * LANE, LANE), LANE), :] = to_col(xrow[it, me_o, pl.ds(b, 1), :])

        @pl.loop(0, nct // group)
        def _(g, it=it):
            def sums(b, acc):
                at = pl.ds(pl.multiple_of(b * chunk, chunk), chunk)
                u = l_col[at, :]
                return tuple(acc[t] + fold(s_ref[g * group + t, at, :] * u, jnp.sum) for t in range(group))

            acc = lax.fori_loop(0, rows // chunk, sums, (jnp.zeros((8, LANE), F32),) * group)
            for t in range(group):
                ct = pl.ds(g * group + t, 1)
                xcol[it, me_m, ct, :] = jnp.sum(acc[t], axis=0, keepdims=True) * v_ref[ct, :]

        finish(start_cols(it))
        csum = sum_over(xcol, it, n_mod)
        v_ref[...] = v_ref[...] / csum
        g_all = g_all + log2(csum)

    colp_ref[...] = (ITERS * (log_mod - log_obs) - g_all) * (EPS * LN2)
    row_totals(ITERS)
    last = start_rows(ITERS)

    @pl.loop(0, nct)
    def _(t):
        at = pl.ds(pl.multiple_of(t * LANE, LANE), LANE)
        o = gath[t // dt, pl.ds(pl.multiple_of(lax.rem(t, dt) * LANE, LANE), LANE), :]
        w = o * to_col(v_ref[pl.ds(t, 1), :])
        hi = w.astype(BF16)
        w_ref[at, 0:feat] = hi
        w_ref[at, feat:2 * feat] = (w - hi.astype(F32)).astype(BF16)

    share = rows // n_obs

    piece = share // 2

    def project(owner, h):
        at = pl.ds(pl.multiple_of(owner * share + h * piece, piece), piece)
        y = jnp.dot(q0_ref[at, :], w_ref[...], preferred_element_type=F32)
        y = y + jnp.dot(q1_ref[at, :], w_ref[...], preferred_element_type=F32)
        return y[:, :feat] + y[:, feat:]

    chips = n_obs // 2
    chip, core = me_o // 2, lax.rem(me_o, 2)
    mate = {"obs": chip * 2 + 1 - core}
    halves, sends = [], []
    for d in list(range(1, chips)) + [0]:
        there = lax.rem(chip + d, chips) * 2
        for h in range(2):
            at = slice(h * piece, (h + 1) * piece)
            part[d, at, :] = project(there + 1 - core, h)
            halves.append(remote(part.at[d, at], half.at[d, at], p_send.at[0, d, h], p_recv.at[0, d, h], mate))
            halves[-1].start()
            mine = project(there + core, h)
            if d:
                halves[-1].wait_recv()
                keep[d - 1, at, :] = mine + half[d, at, :]
                sends.append(remote(keep.at[d - 1, at], mapx.at[d - 1, at], p_send.at[1, d, h], p_recv.at[1, d, h], {"obs": there + core}))
                sends[-1].start()
            else:
                map_ref[at, :] = mine

    finish(last)
    rsum = sum_over(xrow, ITERS, n_obs)
    rowp_ref[...] = (log_obs - ITERS * (log_mod - log_obs) - l1_ref[...] - log2(rsum) + rsq[...]) * (EPS * LN2)
    l1_ref[...] = 1.0 / rsum
    for copy in halves[-2:] + sends:
        copy.wait_recv()
    for b in range(share // LANE):
        at = slice(b * LANE, (b + 1) * LANE)
        y = map_ref[at, :] + half[0, at, :]
        for d in range(1, chips):
            y = y + mapx[d - 1, at, :]
        map_ref[at, :] = y * to_col(l1_ref[pl.ds(me_o * (share // LANE) + b, 1), :])
    for copy in halves + sends:
        copy.wait_send()
    own_sends(lambda copy: copy.wait_send())
    for step in range(1, n_mod):
        each_send(block_at(step), lambda copy: copy.wait_send())


def on_device(n_mod, n_obs, model_days, obs_days):
    rows, feat = model_days.shape
    depth = obs_days.shape[0]
    cols = depth * n_mod
    share = rows // n_obs
    nrb, nct = rows // LANE, cols // LANE
    vmem = pl.BlockSpec(memory_space=pltpu.VMEM)
    dma = pltpu.SemaphoreType.DMA
    mapped, rowp, colp = pl.pallas_call(
        functools.partial(kernel, n_mod, n_obs),
        out_shape=(
            jax.ShapeDtypeStruct((share, feat), F32),
            jax.ShapeDtypeStruct((nrb, LANE), F32),
            jax.ShapeDtypeStruct((nct, LANE), F32),
        ),
        in_specs=[vmem, vmem],
        out_specs=(vmem, vmem, vmem),
        scratch_shapes=[
            pltpu.VMEM((n_mod, depth, feat), F32),
            pltpu.VMEM((rows, 6 * feat), BF16),
            pltpu.VMEM((6 * feat, depth), BF16),
            pltpu.VMEM((1, depth), F32),
            pltpu.VMEM((nct, rows, LANE), F32),
            pltpu.VMEM((rows, cols), BF16),
            pltpu.VMEM((rows, cols), BF16),
            pltpu.VMEM((cols, 2 * feat), BF16),
            pltpu.VMEM((rows, LANE), F32),
            pltpu.VMEM((rows, LANE), F32),
            pltpu.VMEM((rows, LANE), F32),
            pltpu.VMEM((nrb, LANE), F32),
            pltpu.VMEM((nrb, LANE), F32),
            pltpu.VMEM((nct, LANE), F32),
            pltpu.VMEM((nct, LANE), F32),
            pltpu.VMEM((ITERS + 1, n_obs, nrb, LANE), F32),
            pltpu.VMEM((ITERS, n_mod, nct, LANE), F32),
            pltpu.VMEM((n_obs // 2, share, feat), F32),
            pltpu.VMEM((n_obs // 2, share, feat), F32),
            pltpu.VMEM((n_obs // 2 - 1, share, feat), F32),
            pltpu.VMEM((n_obs // 2 - 1, share, feat), F32),
            dma((n_mod + 1,)), dma((n_mod,)),
            dma((ITERS + 1, n_obs)), dma((ITERS + 1, n_obs)),
            dma((ITERS, n_mod)), dma((ITERS, n_mod)),
            dma((2, n_obs // 2, 2)), dma((2, n_obs // 2, 2)),
        ],
        compiler_params=pltpu.CompilerParams(
            collective_id=0, has_side_effects=True, vmem_limit_bytes=56 * 1024 * 1024),
        cost_estimate=pl.CostEstimate(
            flops=20 * rows * cols * feat, bytes_accessed=8 * rows * feat, transcendentals=3 * rows * cols),
    )(model_days, obs_days)
    return mapped, rowp.reshape(rows), colp.reshape(cols)


def solution(mesh):
    n_mod, n_obs = mesh.shape["mod"], mesh.shape["obs"]
    in_specs = (P(("region", "mod"), None), P(("region", "obs", "mod"), None))
    out_specs = (P(("region", "mod", "obs"), None), P(("region", "mod")), P(("region", "obs")))
    return jax.shard_map(
        functools.partial(on_device, n_mod, n_obs), mesh=mesh,
        in_specs=in_specs, out_specs=out_specs, check_vma=False,
    )
```

```python
import functools
import math

import jax
import jax.numpy as jnp
from jax import lax
from jax.experimental import pallas as pl
from jax.experimental.pallas import tpu as pltpu
from jax.sharding import PartitionSpec as P

ITERS = 2
EPS = 0.02
LOG2E = math.log2(math.e)
LN2 = math.log(2.0)
LANE = 128
F32 = jnp.float32
BF16 = jnp.bfloat16


def split3(x):
    a = x.astype(BF16)
    r = x - a.astype(F32)
    b = r.astype(BF16)
    c = (r - b.astype(F32)).astype(BF16)
    return a, b, c


def log2(x):
    return jnp.log(x) * LOG2E


def to_col(row):
    return jnp.broadcast_to(row, (LANE, LANE)).T


def kernel(n_mod, n_obs, model_ref, obs_ref, map_ref, rowp_ref, colp_ref,
           gath, a_ref, b_ref, c_ref, s_ref, q_ref, w_ref, peak_col,
           tot_col, l_col, rsq, l1_ref, m_ref, v_ref, xrow, xcol, part, half, keep, mapx,
           g_send, g_recv, r_send, r_recv, c_send, c_recv, p_send, p_recv):
    rows, feat = model_ref.shape
    depth = obs_ref.shape[0]
    cols = depth * n_mod
    nrb, nct, dt = rows // LANE, cols // LANE, depth // LANE
    scale = LOG2E / EPS
    log_obs = math.log2(cols * n_obs)
    log_mod = math.log2(rows * n_mod)
    me_m, me_o = lax.axis_index("mod"), lax.axis_index("obs")
    mod_peer = lambda k: {"mod": lax.rem(me_m + k, n_mod)}
    obs_peer = lambda k: {"obs": lax.rem(me_o + k, n_obs)}

    barrier = pltpu.get_barrier_semaphore()
    for k in range(1, n_mod):
        pl.semaphore_signal(barrier, inc=1, device_id=mod_peer(k), device_id_type=pl.DeviceIdType.MESH)
    for k in range(1, n_obs):
        pl.semaphore_signal(barrier, inc=1, device_id=obs_peer(k), device_id_type=pl.DeviceIdType.MESH)
    def remote(src, dst, send, recv, peer):
        return pltpu.make_async_remote_copy(
            src_ref=src, dst_ref=dst, send_sem=send, recv_sem=recv,
            device_id=peer, device_id_type=pl.DeviceIdType.MESH)

    @pl.loop(0, nrb)
    def _(b):
        blk = model_ref[pl.ds(pl.multiple_of(b * LANE, LANE), LANE), :]
        sq = blk * blk
        rsq[pl.ds(b, 1), :] = jnp.sum(sq.T, axis=0, keepdims=True) * (scale / feat)
        p0, p1, p2 = split3(blk * (2.0 * scale / feat))
        at = pl.ds(pl.multiple_of(b * LANE, LANE), LANE)
        for t, piece in enumerate((p0, p0, p1, p1, p0, p2)):
            a_ref[at, t * feat:(t + 1) * feat] = piece

    pl.semaphore_wait(barrier, n_mod + n_obs - 2)

    right, left = {"mod": lax.rem(me_m + 1, n_mod)}, {"mod": lax.rem(me_m + n_mod - 1, n_mod)}
    has_right, has_left = me_m < n_mod - 1, me_m > 0
    inside = jnp.logical_and(has_right, has_left)
    n_left, n_right = me_m, n_mod - 1 - me_m
    both = jnp.minimum(n_left, n_right)

    def block_at(j):
        paired = (j - 1) < 2 * both
        far = jnp.where(paired, (j - 1) // 2 + 1, j - both)
        to_left = jnp.where(paired, (j - 1) % 2 == 0, n_left > n_right)
        return jnp.where(to_left, me_m - far, me_m + far)

    def own_to(peer, sem):
        return remote(obs_ref, gath.at[me_m], g_send.at[sem], g_recv.at[me_m], peer)

    def pass_on(block, peer):
        return remote(gath.at[block], gath.at[block], g_send.at[block], g_recv.at[block], peer)

    def each_send(block, act):
        @pl.when(jnp.logical_and(block < me_m, has_right))
        def _():
            act(pass_on(block, right))

        @pl.when(jnp.logical_and(block > me_m, has_left))
        def _():
            act(pass_on(block, left))

    def own_sends(act):
        @pl.when(has_right)
        def _():
            act(own_to(right, me_m))

        @pl.when(has_left)
        def _():
            act(own_to(left, n_mod))

    def arrive(j):
        block = block_at(j)
        pass_on(block, right).wait_recv()
        each_send(block, lambda copy: copy.start())

    own_sends(lambda copy: copy.start())
    gath[me_m] = obs_ref[...]

    mrows = math.gcd(rows, 512)
    for step in range(n_mod):
        if step == 1:
            arrive(1)
        if step and step + 1 < n_mod:
            pl.when(inside)(functools.partial(arrive, step + 1))
        owner = block_at(step) if step else me_m
        for t in range(dt):
            bt = gath[owner, t * LANE:(t + 1) * LANE, :].T
            lanes = slice(t * LANE, (t + 1) * LANE)
            c_ref[:, lanes] = jnp.sum(bt * bt, axis=0, keepdims=True) * (scale / feat)
            p0, p1, p2 = split3(bt)
            for u, piece in enumerate((p0, p1, p0, p1, p2, p0)):
                b_ref[u * feat:(u + 1) * feat, lanes] = piece

        @pl.loop(0, rows // mrows)
        def _(b, owner=owner, step=step):
            at = pl.ds(pl.multiple_of(b * mrows, mrows), mrows)
            x = jnp.dot(a_ref[at, :], b_ref[...], preferred_element_type=F32) - c_ref[...]
            for t in range(dt):
                s_ref[owner * dt + t, at, :] = x[:, t * LANE:(t + 1) * LANE]

        chunk = 64

        @pl.loop(0, rows // chunk, unroll=2)
        def _(b, owner=owner, step=step):
            at = pl.ds(pl.multiple_of(b * chunk, chunk), chunk)
            tiles = [s_ref[owner * dt + t, at, :] for t in range(dt)]
            top = functools.reduce(jnp.maximum, tiles)
            if step:
                old = peak_col[at, :]
                top = jnp.maximum(top, old)
            total = functools.reduce(jnp.add, [jnp.exp2(t - top) for t in tiles])
            if step:
                total = total + tot_col[at, :] * jnp.exp2(old - top)
            peak_col[at, :] = top
            tot_col[at, :] = total

        if step and step + 1 < n_mod:
            pl.when(jnp.logical_not(inside))(functools.partial(arrive, step + 1))

    def start_rows(e):
        copies = []
        for k in range(1, n_obs):
            copies.append(remote(xrow.at[e, me_o], xrow.at[e, me_o], r_send.at[e, k], r_recv.at[e, k], obs_peer(k)))
            copies[-1].start()
        return copies

    def start_cols(e):
        copies = []
        for k in range(1, n_mod):
            copies.append(remote(xcol.at[e, me_m], xcol.at[e, me_m], c_send.at[e, k], c_recv.at[e, k], mod_peer(k)))
            copies[-1].start()
        return copies

    def finish(copies):
        for copy in copies:
            copy.wait_recv()
        for copy in copies:
            copy.wait_send()

    def lse_over(buf, e, n):
        values = [buf[e, d] for d in range(n)]
        top = functools.reduce(jnp.maximum, values)
        return top + log2(functools.reduce(jnp.add, [jnp.exp2(v - top) for v in values]))

    def sum_over(buf, e, n):
        return functools.reduce(jnp.add, [buf[e, d] for d in range(n)])

    def spread(value_ref):
        @pl.loop(0, nrb)
        def _(b):
            l_col[pl.ds(pl.multiple_of(b * LANE, LANE), LANE), :] = to_col(value_ref[pl.ds(b, 1), :])

    @pl.loop(0, nrb)
    def _(b):
        at = pl.ds(pl.multiple_of(b * LANE, LANE), LANE)
        peaks = peak_col[at, :].T
        top = jnp.max(peaks, axis=0, keepdims=True)
        total = jnp.sum(tot_col[at, :].T * jnp.exp2(peaks - top), axis=0, keepdims=True)
        xrow[0, me_o, pl.ds(b, 1), :] = top + log2(total)

    finish(start_rows(0))
    l1_ref[...] = lse_over(xrow, 0, n_obs)
    spread(l1_ref)

    group = 4
    chunk = 128
    share = rows // n_obs
    piece = share // 2

    def fold(x, op):
        return op(x.reshape(chunk // 8, 8, LANE), axis=0)

    @pl.loop(0, nct // group)
    def _(g):
        def peaks(b, acc):
            at = pl.ds(pl.multiple_of(b * chunk, chunk), chunk)
            l = l_col[at, :]
            return tuple(jnp.maximum(acc[t], fold(s_ref[g * group + t, at, :] - l, jnp.max)) for t in range(group))

        acc = lax.fori_loop(0, rows // chunk, peaks, (jnp.full((8, LANE), -jnp.inf, F32),) * group)
        top = [jnp.max(a, axis=0, keepdims=True) for a in acc]

        def sums(b, acc):
            at = pl.ds(pl.multiple_of(b * chunk, chunk), chunk)
            l = l_col[at, :]
            out = []
            for t in range(group):
                q = jnp.exp2(s_ref[g * group + t, at, :] - l - top[t])
                s_ref[g * group + t, at, :] = q
                out.append(acc[t] + fold(q, jnp.sum))
            return tuple(out)

        acc = lax.fori_loop(0, rows // chunk, sums, (jnp.zeros((8, LANE), F32),) * group)
        for t in range(group):
            m_ref[pl.ds(g * group + t, 1), :] = top[t]
            total = jnp.sum(acc[t], axis=0, keepdims=True)
            xcol[0, me_m, pl.ds(g * group + t, 1), :] = top[t] + log2(total)

    finish(start_cols(0))
    g_all = lse_over(xcol, 0, n_mod)
    v_ref[...] = jnp.exp2(m_ref[...] - g_all)

    def row_totals(e):
        @pl.loop(0, nrb)
        def _(b):
            at = pl.ds(pl.multiple_of(b * LANE, LANE), LANE)
            acc = s_ref[0, at, :] * v_ref[0:1, :]
            for t in range(1, nct):
                acc = acc + s_ref[t, at, :] * v_ref[t:t + 1, :]
            xrow[e, me_o, pl.ds(b, 1), :] = jnp.sum(acc.T, axis=0, keepdims=True)

    for it in range(1, ITERS):
        row_totals(it)
        copies = start_rows(it)
        if it == 1:
            @pl.loop(0, rows // chunk)
            def _(b):
                at = pl.ds(pl.multiple_of(b * chunk, chunk), chunk)
                base = lax.div(b, piece // chunk) * (2 * piece) + lax.rem(b, piece // chunk) * chunk
                top = pl.ds(pl.multiple_of(base, chunk), chunk)
                low = pl.ds(pl.multiple_of(base + piece, chunk), chunk)
                for t in range(nct):
                    q = s_ref[t, at, :]
                    hi = q.astype(BF16)
                    q_ref[top, t * LANE:(t + 1) * LANE] = hi
                    q_ref[low, t * LANE:(t + 1) * LANE] = (q - hi.astype(F32)).astype(BF16)
        finish(copies)
        rsum = sum_over(xrow, it, n_obs)
        xrow[it, me_o] = 1.0 / rsum

        @pl.loop(0, nrb)
        def _(b, it=it):
            l_col[pl.ds(pl.multiple_of(b * LANE, LANE), LANE), :] = to_col(xrow[it, me_o, pl.ds(b, 1), :])

        @pl.loop(0, nct // group)
        def _(g, it=it):
            def sums(b, acc):
                at = pl.ds(pl.multiple_of(b * chunk, chunk), chunk)
                u = l_col[at, :]
                return tuple(acc[t] + fold(s_ref[g * group + t, at, :] * u, jnp.sum) for t in range(group))

            acc = lax.fori_loop(0, rows // chunk, sums, (jnp.zeros((8, LANE), F32),) * group)
            for t in range(group):
                ct = pl.ds(g * group + t, 1)
                xcol[it, me_m, ct, :] = jnp.sum(acc[t], axis=0, keepdims=True) * v_ref[ct, :]

        finish(start_cols(it))
        csum = sum_over(xcol, it, n_mod)
        v_ref[...] = v_ref[...] / csum
        g_all = g_all + log2(csum)

    colp_ref[...] = (ITERS * (log_mod - log_obs) - g_all) * (EPS * LN2)
    row_totals(ITERS)
    last = start_rows(ITERS)

    @pl.loop(0, nct)
    def _(t):
        at = pl.ds(pl.multiple_of(t * LANE, LANE), LANE)
        o = gath[t // dt, pl.ds(pl.multiple_of(lax.rem(t, dt) * LANE, LANE), LANE), :]
        w = o * to_col(v_ref[pl.ds(t, 1), :])
        hi = w.astype(BF16)
        w_ref[at, 0:feat] = hi
        w_ref[at, feat:2 * feat] = (w - hi.astype(F32)).astype(BF16)


    def project(owner, h):
        at = pl.ds(pl.multiple_of((owner * 2 + h) * (2 * piece), 2 * piece), 2 * piece)
        y = jnp.dot(q_ref[at, :], w_ref[...], preferred_element_type=F32)
        y = y[:piece] + y[piece:]
        return y[:, :feat] + y[:, feat:]

    chips = n_obs // 2
    chip, core = me_o // 2, lax.rem(me_o, 2)
    mate = {"obs": chip * 2 + 1 - core}
    halves, sends = [], []
    for d in list(range(1, chips)) + [0]:
        there = lax.rem(chip + d, chips) * 2
        for h in range(2):
            at = slice(h * piece, (h + 1) * piece)
            part[d, at, :] = project(there + 1 - core, h)
            halves.append(remote(part.at[d, at], half.at[d, at], p_send.at[0, d, h], p_recv.at[0, d, h], mate))
            halves[-1].start()
            mine = project(there + core, h)
            if d:
                halves[-1].wait_recv()
                keep[d - 1, at, :] = mine + half[d, at, :]
                sends.append(remote(keep.at[d - 1, at], mapx.at[d - 1, at], p_send.at[1, d, h], p_recv.at[1, d, h], {"obs": there + core}))
                sends[-1].start()
            else:
                map_ref[at, :] = mine

    finish(last)
    rsum = sum_over(xrow, ITERS, n_obs)
    rowp_ref[...] = (log_obs - ITERS * (log_mod - log_obs) - l1_ref[...] - log2(rsum) + rsq[...]) * (EPS * LN2)
    l1_ref[...] = 1.0 / rsum
    for copy in halves[-2:] + sends:
        copy.wait_recv()
    for b in range(share // LANE):
        at = slice(b * LANE, (b + 1) * LANE)
        y = map_ref[at, :] + half[0, at, :]
        for d in range(1, chips):
            y = y + mapx[d - 1, at, :]
        map_ref[at, :] = y * to_col(l1_ref[pl.ds(me_o * (share // LANE) + b, 1), :])
    for copy in halves + sends:
        copy.wait_send()
    own_sends(lambda copy: copy.wait_send())
    for step in range(1, n_mod):
        each_send(block_at(step), lambda copy: copy.wait_send())


def on_device(n_mod, n_obs, model_days, obs_days):
    rows, feat = model_days.shape
    depth = obs_days.shape[0]
    cols = depth * n_mod
    share = rows // n_obs
    nrb, nct = rows // LANE, cols // LANE
    vmem = pl.BlockSpec(memory_space=pltpu.VMEM)
    dma = pltpu.SemaphoreType.DMA
    mapped, rowp, colp = pl.pallas_call(
        functools.partial(kernel, n_mod, n_obs),
        out_shape=(
            jax.ShapeDtypeStruct((share, feat), F32),
            jax.ShapeDtypeStruct((nrb, LANE), F32),
            jax.ShapeDtypeStruct((nct, LANE), F32),
        ),
        in_specs=[vmem, vmem],
        out_specs=(vmem, vmem, vmem),
        scratch_shapes=[
            pltpu.VMEM((n_mod, depth, feat), F32),
            pltpu.VMEM((rows, 6 * feat), BF16),
            pltpu.VMEM((6 * feat, depth), BF16),
            pltpu.VMEM((1, depth), F32),
            pltpu.VMEM((nct, rows, LANE), F32),
            pltpu.VMEM((2 * rows, cols), BF16),
            pltpu.VMEM((cols, 2 * feat), BF16),
            pltpu.VMEM((rows, LANE), F32),
            pltpu.VMEM((rows, LANE), F32),
            pltpu.VMEM((rows, LANE), F32),
            pltpu.VMEM((nrb, LANE), F32),
            pltpu.VMEM((nrb, LANE), F32),
            pltpu.VMEM((nct, LANE), F32),
            pltpu.VMEM((nct, LANE), F32),
            pltpu.VMEM((ITERS + 1, n_obs, nrb, LANE), F32),
            pltpu.VMEM((ITERS, n_mod, nct, LANE), F32),
            pltpu.VMEM((n_obs // 2, share, feat), F32),
            pltpu.VMEM((n_obs // 2, share, feat), F32),
            pltpu.VMEM((n_obs // 2 - 1, share, feat), F32),
            pltpu.VMEM((n_obs // 2 - 1, share, feat), F32),
            dma((n_mod + 1,)), dma((n_mod,)),
            dma((ITERS + 1, n_obs)), dma((ITERS + 1, n_obs)),
            dma((ITERS, n_mod)), dma((ITERS, n_mod)),
            dma((2, n_obs // 2, 2)), dma((2, n_obs // 2, 2)),
        ],
        compiler_params=pltpu.CompilerParams(
            collective_id=0, has_side_effects=True, vmem_limit_bytes=56 * 1024 * 1024),
        cost_estimate=pl.CostEstimate(
            flops=20 * rows * cols * feat, bytes_accessed=8 * rows * feat, transcendentals=3 * rows * cols),
    )(model_days, obs_days)
    return mapped, rowp.reshape(rows), colp.reshape(cols)


def solution(mesh):
    n_mod, n_obs = mesh.shape["mod"], mesh.shape["obs"]
    in_specs = (P(("region", "mod"), None), P(("region", "obs", "mod"), None))
    out_specs = (P(("region", "mod", "obs"), None), P(("region", "mod")), P(("region", "obs")))
    return jax.shard_map(
        functools.partial(on_device, n_mod, n_obs), mesh=mesh,
        in_specs=in_specs, out_specs=out_specs, check_vma=False,
    )
```
